32 devices in a mesh: rep: 16 (over z, x, core), fsdp: 2 (over y).
Axes of the slice: x: 2, y: 2, z: 4, core: 2. Of those that a mesh axis runs over, the one named last changes fastest.
Arguments:
- activations: float32 [16384, 960], P(('rep', 'fsdp')), may hold values from -6 to 6
- segments: int32 [16384], P(('rep', 'fsdp')), may hold values from 0 to 47, as said below
- q_weight: bfloat16 [960, 960], P('fsdp'), may hold values from -0.1875 to 0.1875
- k_weight: bfloat16 [960, 320], P('fsdp'), may hold values from -0.1875 to 0.1875
- v_weight: bfloat16 [960, 320], P('fsdp'), may hold values from -0.1875 to 0.1875
- o_weight: bfloat16 [960, 960], P('fsdp'), may hold values from -0.75 to 0.75
- gate_weight: bfloat16 [960, 2560], P('fsdp'), may hold values from -0.1875 to 0.1875
- up_weight: bfloat16 [960, 2560], P('fsdp'), may hold values from -0.1875 to 0.1875
- down_weight: bfloat16 [2560, 960], P('fsdp'), may hold values from -0.125 to 0.125
- attn_gain: bfloat16 [960], P('fsdp'), may hold values from 0.25 to 1.75
- ffn_gain: bfloat16 [960], P('fsdp'), may hold values from 0.25 to 1.75
- out_grad: float32 [16384, 960], P(('rep', 'fsdp')), may hold values from -6 to 6
Outputs:
- output: float32 [16384, 960], P(('rep', 'fsdp'))
- grad_activations: float32 [16384, 960], P(('rep', 'fsdp'))
- grad_q_weight: float32 [960, 960], P('fsdp')
- grad_k_weight: float32 [960, 320], P('fsdp')
- grad_v_weight: float32 [960, 320], P('fsdp')
- grad_o_weight: float32 [960, 960], P('fsdp')
- grad_gate_weight: float32 [960, 2560], P('fsdp')
- grad_up_weight: float32 [960, 2560], P('fsdp')
- grad_down_weight: float32 [2560, 960], P('fsdp')
- grad_attn_gain: float32 [960], P('fsdp')
- grad_ffn_gain: float32 [960], P('fsdp')
The draws below stay inside these ranges and needn't reach their ends.
Inputs may be any that keep to these rules, and one draw needn't show every extreme that they name: `segments`: segment numbers never fall. Sequence s holds documents 3 s, 3 s + 1 and 3 s + 2 in that order; document 3 s + 1 starts within the first 512 tokens of the sequence and ends within its last 512.
All inputs are finite; a program needn't handle non-finite values.
Results may differ from the reference program's by a relative error of at most 0.023.
Values may be sent and summed in bfloat16 or wider, within the bound.
A program may use at most 192 MiB of HBM per device.

```python
import jax
import jax.numpy as jnp
from jax import lax

D = 960
FF = 2560
QH = 15
KVH = 5
HD = 64
TOK_DEV = 512
KEYBLK = 512
SEQ = 1024
SEQS = 16
TOKENS = 16384


def draw_segments(key, part):
    key = jax.random.fold_in(key, 7)
    first_key, second_key = jax.random.split(key)
    lead_end = jax.random.randint(first_key, (SEQS, 1), 1, TOK_DEV)
    tail_start = jax.random.randint(second_key, (SEQS, 1), SEQ - TOK_DEV + 1, SEQ)
    positions = jnp.arange(SEQ, dtype=jnp.int32)[None, :]
    document = (positions >= lead_end).astype(jnp.int32) + (positions >= tail_start).astype(jnp.int32)
    return (document + 3 * jnp.arange(SEQS, dtype=jnp.int32)[:, None]).reshape(TOKENS)


def block_scale(key, shape, pieces, least, largest):
    def one(dim, blocks):
        heights = jax.random.uniform(jax.random.fold_in(jax.random.fold_in(key, 6), dim), (blocks,), jnp.float32, least / len(pieces), largest / len(pieces))
        return jnp.repeat(jnp.exp(heights), shape[dim] // blocks).reshape((-1,) + (1,) * (len(shape) - dim - 1))

    gain = one(*pieces[0])
    for cut in pieces[1:]:
        gain = gain * one(*cut)
    return gain


def normal_values(key, dims, deviation, reach, cuts=(), held_as=jnp.bfloat16):
    loudness = block_scale(key, dims, cuts, -0.22, 0.18) if cuts else 1.0
    array = jax.random.normal(key, dims, jnp.float32) * deviation * loudness
    return jnp.minimum(jnp.maximum(array, -reach), reach).astype(held_as)


def setup_inputs(seed: int = 0) -> dict:
    key_of = jax.random.split(jax.random.key(seed), 13)
    return {
        "activations": normal_values(key_of[0], (TOKENS, D), 1.0, 6.0, ((0, 32),), jnp.float32),
        "segments": draw_segments(jax.random.fold_in(key_of[12], 71), 0),
        "q_weight": normal_values(key_of[2], (D, QH * HD), D ** -0.5, 0.1875, ((0, 2),)),
        "k_weight": normal_values(key_of[3], (D, KVH * HD), D ** -0.5, 0.1875, ((0, 2),)),
        "v_weight": normal_values(key_of[4], (D, KVH * HD), D ** -0.5, 0.1875, ((0, 2),)),
        "o_weight": normal_values(key_of[5], (QH * HD, D), (QH * HD // 16) ** -0.5, 0.75, ((0, 2),)),
        "gate_weight": normal_values(key_of[6], (D, FF), D ** -0.5, 0.1875, ((0, 2),)),
        "up_weight": normal_values(key_of[7], (D, FF), D ** -0.5, 0.1875, ((0, 2),)),
        "down_weight": normal_values(key_of[8], (FF, D), FF ** -0.5, 0.125, ((0, 2),)),
        "attn_gain": jnp.clip(1.0 + 0.15 * jax.random.normal(key_of[9], (D,), jnp.float32), 0.25, 1.75).astype(jnp.bfloat16),
        "ffn_gain": jnp.clip(1.0 + 0.15 * jax.random.normal(key_of[10], (D,), jnp.float32), 0.25, 1.75).astype(jnp.bfloat16),
        "out_grad": normal_values(key_of[11], (TOKENS, D), 1.0, 6.0, ((0, 32),), jnp.float32),
    }


epsilon = 1e-05
rope_base = 100000.0
highest = lax.Precision.HIGHEST

@jax.custom_vjp
def low(v):
    return lax.optimization_barrier(v.astype(jnp.bfloat16)).astype(jnp.float32)

@jax.custom_vjp
def low_back(v):
    return v

def low_keep(v):
    return (low(v), None)

def low_pass(kept, grad):
    return (grad,)

def back_keep(v):
    return (v, None)

def back_low(kept, grad):
    return (low(grad),)
low.defvjp(low_keep, low_pass)
low_back.defvjp(back_keep, back_low)

def rotary_tables(positions):
    exponent = jnp.arange(HD // 2, dtype=jnp.float32) * 2.0 / HD
    inverse = rope_base ** (-exponent)
    angles = positions.astype(jnp.float32)[:, None] * inverse[None, :]
    angles = jnp.concatenate([angles, angles], axis=1)
    return (jnp.cos(angles), jnp.sin(angles))

def rotate(head_values, cosine_table, sine_table):
    half_width = head_values.shape[-1] // 2
    turned = jnp.concatenate([-head_values[..., half_width:], head_values[..., :half_width]], axis=-1)
    return head_values * cosine_table[:, None, :] + turned * sine_table[:, None, :]

def rms_scale(values):
    return lax.rsqrt(lax.optimization_barrier(jnp.mean(values * values, axis=-1, keepdims=True)) + epsilon)

def attend(queries, keys_all, values_all, segment_row):
    length = queries.shape[0]
    softmax_scale = HD ** (-0.5)
    key_positions = jnp.arange(length, dtype=jnp.int32)

    def one_block(block_start):
        block_queries = lax.dynamic_slice_in_dim(queries, block_start, KEYBLK, 0)
        block_segments = lax.dynamic_slice_in_dim(segment_row, block_start, KEYBLK, 0)
        query_positions = block_start + jnp.arange(KEYBLK, dtype=jnp.int32)
        scores = jnp.einsum('tkgd,skd->kgts', block_queries, keys_all, precision=highest) * softmax_scale
        scores = low_back(scores)
        allowed = (block_segments[:, None] == segment_row[None, :]) & (key_positions[None, :] <= query_positions[:, None])
        masked = jnp.where(allowed, scores, -1e+30)
        running_top = lax.optimization_barrier(jnp.max(masked, axis=-1, keepdims=True))
        exponent = jnp.where(allowed, jnp.exp(masked - running_top), 0.0)
        probs_full = exponent / lax.optimization_barrier(jnp.sum(exponent, axis=-1, keepdims=True))
        return jnp.einsum('kgts,skd->tkgd', low(probs_full), values_all, precision=highest)
    starts = (jnp.arange(length // KEYBLK) * KEYBLK).astype(jnp.int32)
    stacked = lax.map(jax.checkpoint(one_block), starts)
    return stacked.reshape(length, QH * HD)

def layer(hidden_rows, params, segment_row, cosine_table, sine_table):
    full_q, full_k, full_v, full_o, full_gate, full_up, full_down, gain_attn, gain_ffn = params
    length = hidden_rows.shape[0]
    normed_one = low(hidden_rows * rms_scale(hidden_rows) * gain_attn)
    q_pre = low_back(jnp.dot(normed_one, full_q, precision=highest))
    k_pre = low_back(jnp.dot(normed_one, full_k, precision=highest))
    v_pre = low_back(jnp.dot(normed_one, full_v, precision=highest))
    queries = low(rotate(q_pre.reshape(length, QH, HD), cosine_table, sine_table))
    queries = queries.reshape(length, KVH, QH // KVH, HD)
    keys_all = low(rotate(k_pre.reshape(length, KVH, HD), cosine_table, sine_table))
    values_all = low(v_pre).reshape(length, KVH, HD)
    attended = attend(queries, keys_all, values_all, segment_row)
    attn_low = low(low_back(attended))
    branch = low_back(jnp.dot(attn_low, full_o, precision=highest))
    middle = hidden_rows + branch
    normed_two = low(middle * rms_scale(middle) * gain_ffn)
    gate_pre = low_back(jnp.dot(normed_two, full_gate, precision=highest))
    up_pre = low_back(jnp.dot(normed_two, full_up, precision=highest))
    hidden_low = low(jax.nn.silu(gate_pre) * up_pre)
    return middle + low_back(jnp.dot(hidden_low, full_down, precision=highest))

def reference(activations, segments, q_weight, k_weight, v_weight, o_weight, gate_weight, up_weight, down_weight, attn_gain, ffn_gain, out_grad):
    params = tuple((weight.astype(jnp.float32) for weight in (q_weight, k_weight, v_weight, o_weight, gate_weight, up_weight, down_weight, attn_gain, ffn_gain)))
    cosine_table, sine_table = rotary_tables(jnp.arange(SEQ, dtype=jnp.int32))
    rows_in = activations.reshape(SEQS, SEQ, D)
    segment_rows = segments.reshape(SEQS, SEQ)
    cotangents = out_grad.reshape(SEQS, SEQ, D)

    def one_sequence(totals, inputs):
        hidden_rows, segment_row, cotangent = inputs

        def forward(rows_now, params_now):
            return layer(rows_now, params_now, segment_row, cosine_table, sine_table)
        result, pullback = jax.vjp(forward, hidden_rows, params)
        grad_rows, grad_params = pullback(cotangent)
        totals = jax.tree.map(jnp.add, totals, grad_params)
        return (totals, (result, grad_rows))
    initial = jax.tree.map(jnp.zeros_like, params)
    totals, (results, grad_rows) = lax.scan(one_sequence, initial, (rows_in, segment_rows, cotangents))
    return (results.reshape(TOKENS, D), grad_rows.reshape(TOKENS, D), totals[0], totals[1], totals[2], totals[3], totals[4], totals[5], totals[6], totals[7], totals[8])
```

```python
import jax
import jax.numpy as jnp
from jax import lax
from jax.sharding import PartitionSpec as P

QH = 15
KVH = 5
HD = 64
KEYBLK = 512


epsilon = 1e-05
rope_base = 100000.0
masked_value = -1e30


def rotary_tables(positions):
    exponent = jnp.arange(HD // 2, dtype=jnp.float32) * 2.0 / HD
    inverse = rope_base ** (-exponent)
    angles = positions.astype(jnp.float32)[:, None] * inverse[None, :]
    angles = jnp.concatenate([angles, angles], axis=1)
    return (jnp.cos(angles), jnp.sin(angles))


def rotate(head_values, cosine_table, sine_table):
    half_width = head_values.shape[-1] // 2
    turned = jnp.concatenate(
        [-head_values[..., half_width:], head_values[..., :half_width]], axis=-1
    )
    return head_values * cosine_table[:, None, :] + turned * sine_table[:, None, :]


def rotate_back(head_grads, cosine_table, sine_table):
    half_width = head_grads.shape[-1] // 2
    spun = head_grads * sine_table[:, None, :]
    return head_grads * cosine_table[:, None, :] + jnp.concatenate(
        [spun[..., half_width:], -spun[..., :half_width]], axis=-1
    )


def rms_scale(values):
    return lax.rsqrt(jnp.mean(values * values, axis=-1, keepdims=True) + epsilon)


def norm_back(inputs, row_scale, gain_full, d_normed):
    weighted = d_normed * gain_full
    gain_term = jnp.sum(d_normed * inputs * row_scale, axis=0)
    d_inputs = row_scale * weighted - inputs * row_scale**3 * jnp.mean(
        weighted * inputs, axis=-1, keepdims=True
    )
    return (d_inputs, gain_term)


def axis_bits(axis):
    size = lax.axis_size(axis)
    bits = []
    bit = 1
    while bit < size:
        bits.append(bit)
        bit *= 2
    return bits


def swap(values, axis, bit):
    size = lax.axis_size(axis)
    return lax.ppermute(values, axis, [(i, i ^ bit) for i in range(size)])


def cut_dim(shape):
    return 1 if (shape[1] // 2) % 128 == 0 else 0


def is_upper(axis, bit):
    return (lax.axis_index(axis) & bit) != 0


def halve(values, dim, axis, bit):
    half = values.shape[dim] // 2
    upper = is_upper(axis, bit).astype(jnp.int32)
    mine = lax.dynamic_slice_in_dim(values, upper * half, half, dim)
    other = lax.dynamic_slice_in_dim(values, (1 - upper) * half, half, dim)
    return mine, other


def join(mine, other, dim, axis, bit):
    upper = is_upper(axis, bit)
    return jnp.where(
        upper,
        jnp.concatenate([other, mine], axis=dim),
        jnp.concatenate([mine, other], axis=dim),
    )


def cut_plan(shape):
    plan = []
    for bit in axis_bits("rep"):
        dim = cut_dim(shape)
        plan.append((bit, dim))
        shape = tuple(n // 2 if i == dim else n for i, n in enumerate(shape))
    return plan


def spread_over_rep(piece, plan):
    for bit, dim in reversed(plan):
        piece = join(piece, swap(piece, "rep", bit), dim, "rep", bit)
    return piece


def gather_shard(shard):
    plan = cut_plan(shard.shape)
    piece = shard
    for bit, dim in plan:
        piece, _ = halve(piece, dim, "rep", bit)
    count = lax.axis_size("fsdp")
    if count == 2:
        other = spread_over_rep(swap(piece, "fsdp", 1), plan)
        return join(shard, other, 0, "fsdp", 1)
    pieces = lax.all_gather(piece, "fsdp", axis=0)
    return jnp.concatenate([spread_over_rep(pieces[i], plan) for i in range(count)], axis=0)


def reduce_shard(whole):
    count = lax.axis_size("fsdp")
    rows = whole.shape[0] // count
    plan = cut_plan((rows, whole.shape[1]))
    held = whole.reshape(count, rows, whole.shape[1])
    held = held.astype(jnp.bfloat16)

    def step(held, dim, axis, bit):
        mine, other = halve(held, dim, axis, bit)
        return mine + swap(other, axis, bit)

    for bit, dim in plan[:1]:
        held = step(held, dim + 1, "rep", bit)
    for bit in reversed(axis_bits("fsdp")):
        held = step(held, 0, "fsdp", bit)
    held = held[0]
    for bit, dim in plan[1:]:
        held = step(held, dim, "rep", bit)
    return spread_over_rep(held, plan)


def body(
    activations,
    segments,
    q_weight,
    k_weight,
    v_weight,
    o_weight,
    gate_weight,
    up_weight,
    down_weight,
    attn_gain,
    ffn_gain,
    out_grad,
):
    rows_here = activations.shape[0]
    my_index = lax.axis_index("fsdp")
    length = rows_here * lax.axis_size("fsdp")
    groups = QH // KVH
    softmax_scale = HD ** (-0.5)
    block_count = length // KEYBLK
    kv_width = KVH * HD
    q_width = QH * HD
    heads_shard = jnp.concatenate([q_weight, k_weight, v_weight, o_weight], axis=1)
    heads_whole = gather_shard(heads_shard)
    full_q = heads_whole[:, :q_width]
    full_k = heads_whole[:, q_width : q_width + kv_width]
    full_v = heads_whole[:, q_width + kv_width : q_width + 2 * kv_width]
    full_o = heads_whole[:, q_width + 2 * kv_width :]
    full_gate = gather_shard(gate_weight)
    full_up = gather_shard(up_weight)
    full_down = gather_shard(down_weight)
    gains = lax.all_gather(jnp.stack([attn_gain, ffn_gain]), "fsdp", axis=1, tiled=True)
    gain_attn, gain_ffn = gains[0], gains[1]
    positions = my_index * rows_here + jnp.arange(rows_here, dtype=jnp.int32)
    last_position = my_index * rows_here + rows_here - 1
    cosine_table, sine_table = rotary_tables(positions)
    scale_one = rms_scale(activations)
    normed_one = (activations * scale_one * gain_attn.astype(jnp.float32)).astype(jnp.bfloat16)
    q_pre = jnp.dot(normed_one, full_q, preferred_element_type=jnp.float32)
    k_pre = jnp.dot(normed_one, full_k, preferred_element_type=jnp.float32)
    v_pre = jnp.dot(normed_one, full_v, preferred_element_type=jnp.float32)
    queries = rotate(q_pre.reshape(rows_here, QH, HD), cosine_table, sine_table).astype(
        jnp.bfloat16
    )
    queries = queries.reshape(rows_here, KVH, groups, HD)
    keys_low = rotate(k_pre.reshape(rows_here, KVH, HD), cosine_table, sine_table).astype(
        jnp.bfloat16
    )
    keys_low = keys_low.reshape(rows_here, KVH * HD)
    values_low = v_pre.astype(jnp.bfloat16)
    both = lax.all_gather(
        jnp.concatenate([keys_low, values_low], axis=1), "fsdp", axis=0, tiled=True
    )
    all_keys, all_values = both[:, :kv_width], both[:, kv_width:]
    all_segments = lax.all_gather(segments, "fsdp", axis=0, tiled=True)

    def block_scores(block_index, key_source, segment_source):
        key_start = block_index * KEYBLK
        key_block = lax.dynamic_slice_in_dim(key_source, key_start, KEYBLK, 0).reshape(
            KEYBLK, KVH, HD
        )
        segment_block = lax.dynamic_slice_in_dim(segment_source, key_start, KEYBLK, 0)
        scores = (
            jnp.einsum("tkgd,skd->kgts", queries, key_block, preferred_element_type=jnp.float32)
            * softmax_scale
        )
        key_positions = key_start + jnp.arange(KEYBLK, dtype=jnp.int32)
        allowed = (segments[:, None] == segment_block[None, :]) & (
            key_positions[None, :] <= positions[:, None]
        )
        return (scores, allowed, key_block)

    def value_rows_of(block_index, value_source):
        return lax.dynamic_slice_in_dim(value_source, block_index * KEYBLK, KEYBLK, 0).reshape(
            KEYBLK, KVH, HD
        )

    def sum_block(block_index, state_pair):

        def sum_visit(state_now):
            running_top, running_sum = state_now
            scores, allowed, key_block = block_scores(block_index, all_keys, all_segments)
            masked = jnp.where(allowed, scores, masked_value)
            new_top = jnp.maximum(running_top, jnp.max(masked, axis=-1))
            exponent = jnp.where(allowed, jnp.exp(masked - new_top[..., None]), 0.0)
            return (
                new_top,
                running_sum * jnp.exp(running_top - new_top) + jnp.sum(exponent, axis=-1),
            )

        return lax.cond(
            block_index * KEYBLK <= last_position,
            sum_visit,
            lambda unchanged: unchanged,
            state_pair,
        )

    start_top = jnp.full((KVH, groups, rows_here), masked_value, jnp.float32)
    start_sum = jnp.zeros((KVH, groups, rows_here), jnp.float32)
    final_top, final_sum = lax.fori_loop(0, block_count, sum_block, (start_top, start_sum))
    log_total = final_top + jnp.log(final_sum)

    def value_block(block_index, accumulated):

        def value_visit(accumulated_now):
            scores, allowed, key_block = block_scores(block_index, all_keys, all_segments)
            probs_full = jnp.where(allowed, jnp.exp(scores - log_total[..., None]), 0.0)
            value_rows = value_rows_of(block_index, all_values)
            return accumulated_now + jnp.einsum(
                "kgts,skd->tkgd",
                probs_full.astype(jnp.bfloat16),
                value_rows,
                preferred_element_type=jnp.float32,
            )

        return lax.cond(
            block_index * KEYBLK <= last_position,
            value_visit,
            lambda unchanged: unchanged,
            accumulated,
        )

    attended = lax.fori_loop(
        0, block_count, value_block, jnp.zeros((rows_here, KVH, groups, HD), jnp.float32)
    )
    attn_low = attended.reshape(rows_here, QH * HD).astype(jnp.bfloat16)
    middle = activations + jnp.dot(attn_low, full_o, preferred_element_type=jnp.float32)
    scale_two = rms_scale(middle)
    normed_two = (middle * scale_two * gain_ffn.astype(jnp.float32)).astype(jnp.bfloat16)
    gate_pre = jnp.dot(normed_two, full_gate, preferred_element_type=jnp.float32)
    up_pre = jnp.dot(normed_two, full_up, preferred_element_type=jnp.float32)
    sigmoid_gate = jax.nn.sigmoid(gate_pre)
    silu_gate = gate_pre * sigmoid_gate
    hidden_low = (silu_gate * up_pre).astype(jnp.bfloat16)
    result = middle + jnp.dot(hidden_low, full_down, preferred_element_type=jnp.float32)
    back_q, back_k, back_v, back_o = full_q, full_k, full_v, full_o
    back_gate, back_up, back_down = full_gate, full_up, full_down
    back_gain_attn, back_gain_ffn = gain_attn, gain_ffn
    key_source, value_source, segment_source = (all_keys, all_values, all_segments)
    cot_low = out_grad.astype(jnp.bfloat16)
    grad_down = jnp.einsum("tf,td->fd", hidden_low, cot_low, preferred_element_type=jnp.float32)
    d_hidden = jnp.einsum("td,fd->tf", cot_low, back_down, preferred_element_type=jnp.float32)
    d_gate = (d_hidden * up_pre * sigmoid_gate * (1.0 + gate_pre * (1.0 - sigmoid_gate))).astype(
        jnp.bfloat16
    )
    d_up = (d_hidden * silu_gate).astype(jnp.bfloat16)
    grad_gate = jnp.einsum("tc,tf->cf", normed_two, d_gate, preferred_element_type=jnp.float32)
    grad_up = jnp.einsum("tc,tf->cf", normed_two, d_up, preferred_element_type=jnp.float32)
    d_normed_two = jnp.einsum("tf,cf->tc", d_gate, back_gate, preferred_element_type=jnp.float32)
    d_normed_two = d_normed_two + jnp.einsum(
        "tf,cf->tc", d_up, back_up, preferred_element_type=jnp.float32
    )
    d_norm_ffn, grad_ffn_term = norm_back(
        middle, scale_two, back_gain_ffn.astype(jnp.float32), d_normed_two
    )
    d_middle = out_grad + d_norm_ffn
    d_branch = d_middle.astype(jnp.bfloat16)
    grad_o = jnp.einsum("tc,td->cd", attn_low, d_branch, preferred_element_type=jnp.float32)
    d_attended = jnp.einsum(
        "td,cd->tc", d_branch, back_o, preferred_element_type=jnp.float32
    ).astype(jnp.bfloat16)
    d_attended = d_attended.reshape(rows_here, KVH, groups, HD)
    row_delta = jnp.einsum("tkgd,tkgd->kgt", d_attended.astype(jnp.float32), attended)

    def grad_block(d_queries, block_index):

        def grad_visit(d_queries_now):
            scores, allowed, key_block = block_scores(block_index, key_source, segment_source)
            value_rows = value_rows_of(block_index, value_source)
            probs_full = jnp.where(allowed, jnp.exp(scores - log_total[..., None]), 0.0)
            d_values = jnp.einsum(
                "kgts,tkgd->skd",
                probs_full.astype(jnp.bfloat16),
                d_attended,
                preferred_element_type=jnp.float32,
            )
            d_probs = jnp.einsum(
                "tkgd,skd->kgts", d_attended, value_rows, preferred_element_type=jnp.float32
            )
            d_scores = (probs_full * (d_probs - row_delta[..., None])).astype(jnp.bfloat16)
            d_queries_now = (
                d_queries_now
                + jnp.einsum(
                    "kgts,skd->tkgd", d_scores, key_block, preferred_element_type=jnp.float32
                )
                * softmax_scale
            )
            d_keys = (
                jnp.einsum("kgts,tkgd->skd", d_scores, queries, preferred_element_type=jnp.float32)
                * softmax_scale
            )
            return (
                d_queries_now,
                (d_keys.reshape(KEYBLK, KVH * HD), d_values.reshape(KEYBLK, KVH * HD)),
            )

        def skip(d_queries_now):
            empty_rows = jnp.zeros((KEYBLK, KVH * HD), jnp.float32)
            return (d_queries_now, (empty_rows, empty_rows))

        return lax.cond(block_index * KEYBLK <= last_position, grad_visit, skip, d_queries)

    start_grads = jnp.zeros((rows_here, KVH, groups, HD), jnp.float32)
    d_queries, (key_terms, value_terms) = lax.scan(
        grad_block, start_grads, jnp.arange(block_count, dtype=jnp.int32)
    )
    key_terms = key_terms.reshape(length, KVH * HD)
    value_terms = value_terms.reshape(length, KVH * HD)
    both_terms = jnp.concatenate([key_terms, value_terms], axis=1).astype(jnp.bfloat16)
    both_sum = lax.psum_scatter(both_terms, "fsdp", scatter_dimension=0, tiled=True)
    d_keys_sum = both_sum[:, :kv_width].astype(jnp.float32)
    d_values_sum = both_sum[:, kv_width:].astype(jnp.float32)
    dq_low = (
        rotate_back(d_queries.reshape(rows_here, QH, HD), cosine_table, sine_table)
        .astype(jnp.bfloat16)
        .reshape(rows_here, QH * HD)
    )
    dk_low = (
        rotate_back(d_keys_sum.reshape(rows_here, KVH, HD), cosine_table, sine_table)
        .astype(jnp.bfloat16)
        .reshape(rows_here, KVH * HD)
    )
    dv_low = d_values_sum.astype(jnp.bfloat16)
    grad_q = jnp.einsum("tc,tq->cq", normed_one, dq_low, preferred_element_type=jnp.float32)
    grad_k = jnp.einsum("tc,tq->cq", normed_one, dk_low, preferred_element_type=jnp.float32)
    grad_v = jnp.einsum("tc,tq->cq", normed_one, dv_low, preferred_element_type=jnp.float32)
    d_normed_one = jnp.einsum("tq,cq->tc", dq_low, back_q, preferred_element_type=jnp.float32)
    d_normed_one = d_normed_one + jnp.einsum(
        "tq,cq->tc", dk_low, back_k, preferred_element_type=jnp.float32
    )
    d_normed_one = d_normed_one + jnp.einsum(
        "tq,cq->tc", dv_low, back_v, preferred_element_type=jnp.float32
    )
    d_norm_attn, grad_attn_term = norm_back(
        activations, scale_one, back_gain_attn.astype(jnp.float32), d_normed_one
    )
    grad_activations = d_middle + d_norm_attn
    down_total = reduce_shard(grad_down).astype(jnp.float32)
    gate_total = reduce_shard(grad_gate).astype(jnp.float32)
    up_total = reduce_shard(grad_up).astype(jnp.float32)
    heads_grad = jnp.concatenate([grad_q, grad_k, grad_v, grad_o], axis=1)
    heads_total = reduce_shard(heads_grad).astype(jnp.float32)
    gain_terms = jnp.stack([grad_attn_term, grad_ffn_term]).astype(jnp.bfloat16)
    gain_share = lax.psum_scatter(gain_terms, "fsdp", scatter_dimension=1, tiled=True)
    gain_total = lax.psum(gain_share, "rep").astype(jnp.float32)
    totals = (
        heads_total[:, :q_width],
        heads_total[:, q_width : q_width + kv_width],
        heads_total[:, q_width + kv_width : q_width + 2 * kv_width],
        heads_total[:, q_width + 2 * kv_width :],
        gate_total,
        up_total,
        down_total,
        gain_total[0],
        gain_total[1],
    )
    return (
        result,
        grad_activations,
        totals[0],
        totals[1],
        totals[2],
        totals[3],
        totals[4],
        totals[5],
        totals[6],
        totals[7],
        totals[8],
    )


def solution(mesh):
    placed = (
        P(("rep", "fsdp"), None),
        P(("rep", "fsdp")),
        P("fsdp", None),
        P("fsdp", None),
        P("fsdp", None),
        P("fsdp", None),
        P("fsdp", None),
        P("fsdp", None),
        P("fsdp", None),
        P("fsdp"),
        P("fsdp"),
        P(("rep", "fsdp"), None),
    )
    return jax.shard_map(
        body,
        mesh=mesh,
        in_specs=placed,
        out_specs=(
            P(("rep", "fsdp"), None),
            P(("rep", "fsdp"), None),
            P("fsdp", None),
            P("fsdp", None),
            P("fsdp", None),
            P("fsdp", None),
            P("fsdp", None),
            P("fsdp", None),
            P("fsdp", None),
            P("fsdp"),
            P("fsdp"),
        ),
        check_vma=False,
    )
```
